256 devices in a mesh: rep: 16 (over x, y), seq: 16 (over z, core).
Axes of the slice: x: 4, y: 4, z: 8, core: 2. Of those that a mesh axis runs over, the one named last changes fastest.
Arguments:
- queries: bfloat16 [16, 2048, 4096], P('rep', 'seq'), may hold values from -6 to 6
- key_rows: bfloat16 [16, 2048, 4096], P('rep', 'seq'), may hold values from -6 to 6
- value_rows: bfloat16 [16, 2048, 4096], P('rep', 'seq'), may hold values from -6 to 6
- cotangent: bfloat16 [16, 2048, 3584], P('rep', 'seq'), may hold values from -0.09375 to 0.09375
- numerators: bfloat16 [16, 4096, 3584], P('rep', 'seq'), may hold values from -6 to 6
- push_weights: float32 [16], P('rep'), may hold values from 0.5 to 2
- doc_ids: int32 [16, 2048], P('rep'), may hold values from 0 to 3, never falling along the last dimension, each value on 1 to 1024 neighbouring positions
- out_links: int32 [16, 16], replicated, may hold values from 0 to 1, as said below
- denominators: int32 [16], replicated, may hold values from 2 to 6, as said below
Outputs:
- query_grads: bfloat16 [16, 2048, 4096], P('rep', 'seq')
- key_grads: bfloat16 [16, 2048, 4096], P('rep', 'seq')
- value_grads: bfloat16 [16, 2048, 4096], P('rep', 'seq')
- mixed_numerators: bfloat16 [16, 4096, 3584], P('rep', 'seq')
- mixed_weights: float32 [16], P('rep')
The draws below stay inside these ranges and needn't reach their ends.
Inputs may be any that keep to these rules, and one draw needn't show every extreme that they name: out_links[r, c] is 1 only where c = (r + 2^b) mod 16 for some b with 2^b < 16; every replica has one or more out-neighbours. denominators[r] is one or two more than the number of out-neighbours of replica r.
All inputs are finite; a program needn't handle non-finite values.
Results may differ from the reference program's by a relative error of at most 0.035.
Values may be sent and summed in bfloat16 or wider, within the bound.
A program may use at most 128 MiB of HBM per device.

```python
import math
import jax
import jax.numpy as jnp
import numpy as np
from jax import lax

HEAD_DIM = 128
HEADS = 32
OUTW = 3584
DOCS = 4
SEQ_LEN = 2048
FEATS = 4096
REPLICAS = 16


def graph_parts(key):
    levels = REPLICAS.bit_length() - 1
    chosen = jax.random.randint(jax.random.fold_in(key, 21), (REPLICAS, levels), 0, 2)
    forced = jax.random.randint(jax.random.fold_in(key, 22), (REPLICAS, 1), 0, levels)
    single = (jnp.arange(levels)[None, :] == forced).astype(jnp.int32)
    heavy = jax.random.randint(jax.random.fold_in(key, 23), (), 0, REPLICAS)
    light = (heavy + jax.random.randint(jax.random.fold_in(key, 24), (), 1, REPLICAS)) % REPLICAS
    rows = jnp.arange(REPLICAS)[:, None]
    link_bits = jnp.maximum(chosen, single)
    link_bits = jnp.where(rows == light, single, link_bits)
    link_bits = jnp.where(rows == heavy, jnp.ones_like(link_bits), link_bits)
    return (link_bits, heavy, light)


def draw_out_links(key, part):
    link_bits, heavy, light = graph_parts(key)
    levels = REPLICAS.bit_length() - 1
    sources = jnp.arange(REPLICAS)
    adjacency = jnp.zeros((REPLICAS, REPLICAS), jnp.int32)
    for bit_level in range(levels):
        target = (sources + 2 ** bit_level) % REPLICAS
        adjacency = adjacency + link_bits[:, bit_level][:, None] * (sources[None, :] == target[:, None]).astype(jnp.int32)
    return adjacency


def draw_denominators(key, part):
    link_bits, heavy, light = graph_parts(key)
    key = jax.random.fold_in(key, 5)
    surplus = jax.random.randint(key, (REPLICAS,), 1, 3)
    rows = jnp.arange(REPLICAS)
    surplus = jnp.where(rows == heavy, 2, jnp.where(rows == light, 1, surplus))
    return jnp.sum(link_bits, axis=1) + surplus


def draw_queries(key, part):
    key = jax.random.fold_in(key, 1)
    shape = (REPLICAS, SEQ_LEN, FEATS)
    result = jnp.clip(jax.random.normal(key, shape, jnp.float32), -6.0, 6.0)
    return result.astype(jnp.bfloat16)


def draw_key_rows(key, part):
    key = jax.random.fold_in(key, 2)
    shape = (REPLICAS, SEQ_LEN, FEATS)
    result = jnp.clip(jax.random.normal(key, shape, jnp.float32), -6.0, 6.0)
    return result.astype(jnp.bfloat16)


def block_scale(stream_key, dims, cuts, low, high):
    gain = 1.0
    for position, blocks in cuts:
        draws = jax.random.uniform(jax.random.fold_in(jax.random.fold_in(stream_key, 6), position), (blocks,), jnp.float32, low / len(cuts), high / len(cuts))
        gain = gain * jnp.repeat(jnp.exp(draws), dims[position] // blocks).reshape((-1,) + (1,) * (len(dims) - 1 - position))
    return gain


def split_up(number_of, total, reach, skew):
    loads = [(1 << 20) // math.isqrt(grade ** skew) + 1 for grade in range(2, number_of + 1)]
    spare, holding = total - reach - (number_of - 1), [1] * (number_of - 1)
    while spare > 0:
        candidates = [i for i in range(number_of - 1) if holding[i] < reach]
        whole, left = sum([loads[i] for i in candidates]), spare
        for i in candidates:
            extra = min(reach - holding[i], max(1, left * loads[i] // whole), spare)
            holding[i] = holding[i] + extra
            spare = spare - extra
    return np.array([reach] + holding)


def ragged(own_key, number_of, total, bound, lean):
    if number_of == 2:
        one = jax.random.randint(own_key, (), max(1, total - bound), min(bound, total - 1) + 1)
        return jnp.stack([one, total - one])
    sizes = jnp.asarray(split_up(number_of, total, bound, lean), jnp.int32)
    twos = (number_of - 1) // 2
    donor, sink = sizes[1:1 + 2 * twos:2], sizes[2:2 + 2 * twos:2]
    room = jnp.minimum(donor - 1, bound - sink)
    passed = jax.random.randint(jax.random.fold_in(own_key, 1), (twos,), 0, 1 << 20) % (room + 1)
    sizes = sizes.at[1:1 + 2 * twos:2].set(donor - passed).at[2:2 + 2 * twos:2].set(sink + passed)
    return sizes[jax.random.permutation(jax.random.fold_in(own_key, 2), number_of)]


def gaussian(key, extent, scale, limit, cuts=(), kind=jnp.bfloat16):
    entries = jax.random.normal(key, extent, jnp.float32) * scale
    if len(cuts) > 0:
        entries = block_scale(key, extent, cuts, -0.22, 0.18) * entries
    return jnp.clip(entries, min=-limit, max=limit).astype(kind)


def setup_inputs(seed: int = 0) -> dict:
    streams_of = jax.random.split(jax.random.key(seed), 10)
    queries = draw_queries(jax.random.fold_in(streams_of[9], 71), 0)
    key_rows = draw_key_rows(jax.random.fold_in(streams_of[9], 71), 0)
    value_rows = gaussian(streams_of[2], (REPLICAS, SEQ_LEN, FEATS), 1.0, 6.0, ((0, 16), (1, 16)))
    cotangent = gaussian(streams_of[3], (REPLICAS, SEQ_LEN, OUTW), OUTW ** -0.5, 0.09375, ((0, 16), (1, 16)))
    numerators = gaussian(streams_of[4], (REPLICAS, FEATS, OUTW), 1.0, 6.0, ((0, 16), (1, 16)))
    push_weights = jnp.clip(jnp.exp(math.log(2.0) - 1.3862944 * jax.random.uniform(streams_of[5], (REPLICAS,), jnp.float32) ** block_scale(streams_of[5], (REPLICAS,), ((0, 16),), -0.2, 0.2)), 0.5, 2.0)
    doc_ids = jax.vmap(lambda own: jnp.searchsorted(jnp.cumsum(ragged(own, DOCS, SEQ_LEN, SEQ_LEN // 2, 0)), jnp.arange(SEQ_LEN), side="right"))(jax.random.split(streams_of[6], REPLICAS)).reshape((REPLICAS, SEQ_LEN)).astype(jnp.int32)
    out_links = draw_out_links(jax.random.fold_in(streams_of[9], 71), 0)
    denominators = draw_denominators(jax.random.fold_in(streams_of[9], 71), 0)
    return dict(queries=queries, key_rows=key_rows, value_rows=value_rows, cotangent=cotangent, numerators=numerators, push_weights=push_weights, doc_ids=doc_ids, out_links=out_links, denominators=denominators)


step_size = 3.0

def head_pass(query_head, key_head, value_head, weight_head, cotangent_rows, doc_row):
    scale_factor = 1.0 / math.sqrt(HEAD_DIM)
    positions = jnp.arange(SEQ_LEN)
    allowed = (positions[None, :] <= positions[:, None]) & (doc_row[None, :] == doc_row[:, None])
    scores = jnp.dot(query_head, key_head.T, preferred_element_type=jnp.float32) * scale_factor
    scores = jnp.where(allowed, scores, -jnp.inf)
    row_peak = lax.optimization_barrier(jnp.max(scores, axis=1, keepdims=True))
    exponent = jnp.exp(scores - row_peak)
    probs_bf = (exponent / lax.optimization_barrier(jnp.sum(exponent, axis=1, keepdims=True))).astype(jnp.bfloat16)
    attended = jnp.dot(probs_bf, value_head, preferred_element_type=jnp.float32).astype(jnp.bfloat16)
    gradient = jnp.dot(attended.T, cotangent_rows, preferred_element_type=jnp.float32)
    grad_attn = jnp.dot(cotangent_rows, weight_head.T, preferred_element_type=jnp.float32).astype(jnp.bfloat16)
    value_grad = jnp.dot(probs_bf.T, grad_attn, preferred_element_type=jnp.float32).astype(jnp.bfloat16)
    grad_probs = jnp.dot(grad_attn, value_head.T, preferred_element_type=jnp.float32)
    centre = lax.optimization_barrier(jnp.sum(grad_attn.astype(jnp.float32) * attended.astype(jnp.float32), axis=1))
    grad_scores = (probs_bf.astype(jnp.float32) * (grad_probs - centre[:, None])).astype(jnp.bfloat16)
    query_grad = (jnp.dot(grad_scores, key_head, preferred_element_type=jnp.float32) * scale_factor).astype(jnp.bfloat16)
    key_grad = (jnp.dot(grad_scores.T, query_head, preferred_element_type=jnp.float32) * scale_factor).astype(jnp.bfloat16)
    return (query_grad, key_grad, value_grad, gradient)

def replica_pass(inputs):
    query_all, key_all, value_all, cotangent_rows, numer_tile, weight_value, doc_row = inputs
    debiased = (numer_tile.astype(jnp.float32) / weight_value).astype(jnp.bfloat16)
    query_heads = query_all.reshape(SEQ_LEN, HEADS, HEAD_DIM).transpose(1, 0, 2)
    key_heads = key_all.reshape(SEQ_LEN, HEADS, HEAD_DIM).transpose(1, 0, 2)
    value_heads = value_all.reshape(SEQ_LEN, HEADS, HEAD_DIM).transpose(1, 0, 2)
    weight_heads = debiased.reshape(HEADS, HEAD_DIM, OUTW)

    def one_head(head_inputs):
        return head_pass(head_inputs[0], head_inputs[1], head_inputs[2], head_inputs[3], cotangent_rows, doc_row)
    query_grad, key_grad, value_grad, gradient = lax.map(one_head, (query_heads, key_heads, value_heads, weight_heads))
    query_grad = query_grad.transpose(1, 0, 2).reshape(SEQ_LEN, FEATS)
    key_grad = key_grad.transpose(1, 0, 2).reshape(SEQ_LEN, FEATS)
    value_grad = value_grad.transpose(1, 0, 2).reshape(SEQ_LEN, FEATS)
    return (query_grad, key_grad, value_grad, gradient.reshape(FEATS, OUTW))

def reference(queries, key_rows, value_rows, cotangent, numerators, push_weights, doc_ids, out_links, denominators):
    query_grads, key_grads, value_grads, gradients = lax.map(replica_pass, (queries, key_rows, value_rows, cotangent, numerators, push_weights, doc_ids))
    half_step = numerators.astype(jnp.float32) - step_size * gradients
    links = out_links.astype(jnp.float32)
    den_values = denominators.astype(jnp.float32)
    kept = 1.0 - lax.optimization_barrier(jnp.sum(links, axis=1)) / den_values
    sending = (half_step / den_values[:, None, None]).astype(jnp.bfloat16)

    def mix_target(target):
        column = out_links[:, target].astype(jnp.bfloat16)
        incoming = jnp.einsum('r,rfo->fo', column, sending, preferred_element_type=jnp.float32)
        return (kept[target] * half_step[target] + incoming).astype(jnp.bfloat16)
    mixed_numerators = lax.map(mix_target, jnp.arange(REPLICAS))
    mixed_weights = kept * push_weights + jnp.dot(links.T, push_weights / den_values, precision=lax.Precision.HIGHEST)
    return (query_grads, key_grads, value_grads, mixed_numerators, mixed_weights)
```

```python
import math

import jax
import jax.numpy as jnp
from jax import lax
from jax.experimental import pallas as pl
from jax.experimental.pallas import tpu as pltpu
from jax.sharding import PartitionSpec as P

HD = 128
SEQ = 2048
TOK = 128
OUTW = 3584
FW = 256
REACH = 4
WIN = REACH + 1
PAD = REACH * 256
CH = 256
NCH = OUTW // CH
STEP_SIZE = 3.0
SCALE = 1.0 / math.sqrt(HD)
EXP2_SCALE = SCALE * math.log2(math.e)
NEG = -1e30
MESH = pl.DeviceIdType.MESH
BF = jnp.bfloat16
F32 = jnp.float32


def mod(a, n):
    return lax.rem(a, n)


def dot_nn(a, b):
    return lax.dot_general(a, b, (((1,), (0,)), ((), ())), preferred_element_type=F32)


def dot_nt(a, b):
    return lax.dot_general(a, b, (((1,), (1,)), ((), ())), preferred_element_type=F32)


def rows(start, size):
    return pl.ds(pl.multiple_of(start, size), size)


def kernel(
    q_ref, k_ref, v_ref, cot_ref, num_ref, doc_ref, pw_ref, links_ref, den_ref,
    dq_out, dk_out, dv_out, mix_out, w_out,
    qh, kp, vp, kt, vt, pb, sbuf, ot, cotb, numb, deb, acc, dqb, dkb, dvb, dcol,
    rb, mixb, wsend, wrecv,
    loc_sem, in_send, in_recv, ring_send, ring_recv, sib_send, sib_recv,
    out_send, out_recv, push_send, push_recv, wp_send, wp_recv, mix_sem,
):
    rep = lax.axis_index("rep")
    me = lax.axis_index("seq")
    x, y = lax.div(rep, 4), mod(rep, 4)
    z, core = lax.div(me, 2), mod(me, 2)
    way = 1 - 2 * core
    sibling = (rep, z * 2 + 1 - core)
    ring_next = (rep, mod(z + way + 8, 8) * 2 + core)

    def at_xy(dx, dy):
        return (mod(x + dx + 4, 4) * 4 + mod(y + dy + 4, 4), me)

    push_to = (at_xy(0, 1), at_xy(0, 2), at_xy(2, 0), at_xy(1, 0))

    barrier = pltpu.get_barrier_semaphore()
    for step in range(1, 16):
        pl.semaphore_signal(
            barrier, inc=1, device_id=(rep, mod(me + step, 16)), device_id_type=MESH
        )
    for dx, dy in ((0, 1), (0, 2), (0, 3), (1, 0), (2, 0), (3, 0)):
        pl.semaphore_signal(barrier, inc=1, device_id=at_xy(dx, dy), device_id_type=MESH)
    pl.semaphore_wait(barrier, 21)

    def remote(src, dst, send, recv, device):
        return pltpu.make_async_remote_copy(
            src_ref=src, dst_ref=dst, send_sem=send, recv_sem=recv, device_id=device,
            device_id_type=MESH,
        )

    heads_in = ((q_ref, qh, 0), (k_ref, kp, PAD), (v_ref, vp, PAD))

    def in_copy(t, dst, src):
        source, target, base = heads_in[t]
        return remote(
            source.at[:, rows(dst * FW, FW)],
            target.at[pl.ds(pl.multiple_of(base + src * TOK, TOK), TOK), :],
            in_send.at[t, dst], in_recv.at[t, src], (rep, dst),
        )

    def in_own(t):
        source, target, base = heads_in[t]
        return pltpu.make_async_copy(
            source.at[:, rows(me * FW, FW)],
            target.at[pl.ds(pl.multiple_of(base + me * TOK, TOK), TOK), :],
            loc_sem.at[t],
        )

    own_cot = pltpu.make_async_copy(cot_ref, cotb.at[rows(me * TOK, TOK), :], loc_sem.at[3])
    own_num = pltpu.make_async_copy(num_ref, numb, loc_sem.at[4])

    def send_in(step, carry):
        dst = mod(me + step, 16)
        for t in range(3):
            in_copy(t, dst, me).start()
        return carry

    own_num.start()
    own_cot.start()
    lax.fori_loop(1, 16, send_in, 0)
    for t in range(3):
        in_own(t).start()

    def ring_block(step):
        return mod(z - way * step + 8, 8) * 2 + core

    def sib_block(step):
        return mod(z + way * step + 8, 8) * 2 + 1 - core

    def half_rows(block, sub):
        return cotb.at[pl.ds(pl.multiple_of(block * TOK + sub * 64, 64), 64), :]

    def ring_copy(step, sub):
        piece = half_rows(ring_block(step), sub)
        return remote(piece, piece, ring_send.at[step, sub], ring_recv.at[step + 1, sub], ring_next)

    def ring_arrival(step, sub):
        piece = half_rows(ring_block(step), sub)
        return remote(piece, piece, ring_send.at[step, sub], ring_recv.at[step, sub], ring_next)

    def sib_copy(step, sub):
        piece = half_rows(ring_block(step), sub)
        return remote(piece, piece, sib_send.at[step, sub], sib_recv.at[step, sub], sibling)

    def sib_arrival(step, sub):
        piece = half_rows(sib_block(step), sub)
        return remote(piece, piece, sib_send.at[step, sub], sib_recv.at[step, sub], sibling)

    own_cot.wait()
    for sub in range(2):
        ring_copy(0, sub).start()
        sib_copy(0, sub).start()

    kp[0:PAD, :] = jnp.zeros((PAD, FW), BF)
    vp[0:PAD, :] = jnp.zeros((PAD, FW), BF)
    dcol[0:PAD, :] = jnp.full((PAD, 128), -1.0, F32)

    def zero_acc(i, carry):
        acc[rows(i * 256, 256), :] = jnp.zeros((256, FW), F32)
        return carry

    lax.fori_loop(0, acc.shape[0] // 256, zero_acc, 0)

    def doc_columns(i, carry):
        part = doc_ref[:, rows(i * 128, 128)].astype(F32)
        dcol[pl.ds(pl.multiple_of(PAD + i * 128, 128), 128), :] = jnp.broadcast_to(
            part, (128, 128)
        ).T
        return carry

    lax.fori_loop(0, SEQ // 128, doc_columns, 0)
    own_num.wait()
    inv_weight = 1.0 / jnp.full((1, CH), pw_ref[0], F32)

    def debias(j, carry):
        cols = rows(j * CH, CH)
        deb[:, cols] = (numb[:, cols].astype(F32) * inv_weight).astype(BF)
        return carry

    lax.fori_loop(0, NCH, debias, 0)

    def wait_in(step, carry):
        src = mod(me - step + 16, 16)
        for t in range(3):
            in_copy(t, mod(me + step, 16), src).wait_recv()
        return carry

    for t in range(3):
        in_own(t).wait()
    lax.fori_loop(1, 16, wait_in, 0)

    def flip(i, carry):
        cols = rows(i * 256, 256)
        kt[:, cols] = kp[cols, :].T
        vt[:, cols] = vp[cols, :].T
        return carry

    lax.fori_loop(0, (PAD + SEQ) // 256, flip, 0)

    later_key = lax.broadcasted_iota(jnp.int32, (256, 256), 0) <= lax.broadcasted_iota(
        jnp.int32, (256, 256), 1
    )

    def forward(a):
        doc_q = doc_ref[:, rows(a * 256, 256)].astype(F32)
        for h in range(2):
            feats = slice(h * HD, (h + 1) * HD)
            qa = qh[rows(a * 256, 256), feats]
            peak = jnp.full((1, 256), NEG, F32)
            for c in range(WIN):
                keys = rows((a + c) * 256, 256)
                scores = dot_nt(kp[keys, feats], qa)
                dk_col = dcol[keys, :]
                allowed = jnp.concatenate([dk_col, dk_col], axis=1) == doc_q
                if c == REACH:
                    allowed = allowed & later_key
                scores = jnp.where(allowed, scores, NEG)
                sbuf[h, c * 256:(c + 1) * 256, :] = scores
                peak = jnp.maximum(peak, jnp.max(scores, axis=0, keepdims=True))
            total = jnp.zeros((1, 256), F32)
            for c in range(WIN):
                part = slice(c * 256, (c + 1) * 256)
                expo = jnp.exp2((sbuf[h, part, :] - peak) * EXP2_SCALE)
                sbuf[h, part, :] = expo
                total = total + jnp.sum(expo, axis=0, keepdims=True)
            inv_total = 1.0 / total
            out = jnp.zeros((HD, 256), F32)
            for c in range(WIN):
                probs = (sbuf[h, c * 256:(c + 1) * 256, :] * inv_total).astype(BF)
                pb[rows(((a * 2 + h) * WIN + c) * 256, 256), :] = probs
                out = out + dot_nn(vt[feats, rows((a + c) * 256, 256)], probs)
            ot[feats, rows(a * 256, 256)] = out.astype(BF)

    def out_copy(t, dst, src):
        source, target = ((dqb, dq_out), (dkb, dk_out), (dvb, dv_out))[t]
        return remote(
            source.at[rows(dst * TOK, TOK), :], target.at[:, rows(src * FW, FW)],
            out_send.at[t, dst], out_recv.at[t, src], (rep, dst),
        )

    def out_own(t):
        source, target = ((dqb, dq_out), (dkb, dk_out), (dvb, dv_out))[t]
        return pltpu.make_async_copy(
            source.at[rows(me * TOK, TOK), :], target.at[:, rows(me * FW, FW)], loc_sem.at[5 + t]
        )

    def backward(a, half):
        device = a * 2 + half
        tok = rows(device * TOK, TOK)
        lanes = slice(half * TOK, (half + 1) * TOK)
        grad = dot_nt(deb[...], cotb[tok, :]).astype(BF)
        for h in range(2):
            feats = slice(h * HD, (h + 1) * HD)
            go = grad[feats, :]
            centre = jnp.sum(
                go.astype(F32) * ot[feats, tok].astype(F32), axis=0, keepdims=True
            )
            qa = qh[tok, feats]
            dq = jnp.zeros((HD, TOK), F32)
            for c in range(WIN):
                keys = rows((a + c) * 256, 256)
                probs = pb[rows(((a * 2 + h) * WIN + c) * 256, 256), lanes]
                grad_probs = dot_nn(vp[keys, feats], go)
                grad_scores = (probs.astype(F32) * (grad_probs - centre)).astype(BF)
                k_rows = keys
                v_rows = pl.ds(pl.multiple_of(PAD + SEQ + (a + c) * 256, 256), 256)
                acc[k_rows, feats] += dot_nn(grad_scores, qa)
                acc[v_rows, feats] += dot_nt(probs, go)
                dq = dq + dot_nn(kt[feats, keys], grad_scores)
            dqb[tok, feats] = (dq * SCALE).T.astype(BF)

        @pl.when(device != me)
        def _():
            out_copy(0, device, me).start()

        @pl.when(device == me)
        def _():
            out_own(0).start()

    def ring_step(s, carry):
        before = mod(z - s + 8, 8)
        after = mod(z + s, 8)

        def take(sub):
            @pl.when(s > 0)
            def _():
                ring_arrival(s, sub).wait_recv()

                @pl.when(s < 7)
                def _():
                    ring_copy(s, sub).start()

                sib_copy(s, sub).start()

        take(0)

        @pl.when(s <= 4)
        def _():
            forward(before)

        take(1)

        @pl.when((s >= 1) & (s <= 3))
        def _():
            forward(after)

        for sub in range(2):
            sib_arrival(s, sub).wait_recv()
        backward(before, 0)
        backward(after, 1)
        return carry

    lax.fori_loop(0, 8, ring_step, 0)

    def finish(i, carry):
        dst = mod(me + i, 16)
        tok = rows(dst * TOK, TOK)
        dkb[tok, :] = (
            acc[pl.ds(pl.multiple_of(PAD + dst * TOK, TOK), TOK), :] * SCALE
        ).astype(BF)
        dvb[tok, :] = acc[
            pl.ds(pl.multiple_of(2 * PAD + SEQ + dst * TOK, TOK), TOK), :
        ].astype(BF)

        @pl.when(i > 0)
        def _():
            out_copy(1, dst, me).start()
            out_copy(2, dst, me).start()

        @pl.when(i == 0)
        def _():
            out_own(1).start()
            out_own(2).start()

        return carry

    lax.fori_loop(0, 16, finish, 0)

    link = [links_ref[rep, mod(rep + off, 16)].astype(F32) for off in (1, 2, 8, 4)]
    inv_den = 1.0 / jnp.full((1, CH), den_ref[rep].astype(F32), F32)
    links_out = links_ref[rep, 0]
    for col in range(1, 16):
        links_out = links_out + links_ref[rep, col]
    kept = 1.0 - jnp.full((1, CH), links_out.astype(F32), F32) * inv_den
    from_1 = jnp.where(y >= 1, 1.0, 0.0)
    from_2 = jnp.where(y >= 2, 1.0, 0.0)
    carry_1 = jnp.where(y == 0, 1.0, 0.0)
    carry_2 = jnp.where(y <= 1, 1.0, 0.0)

    def send_rows(msg, j):
        return rows((msg * NCH + j) * 256, 256)

    def push_copy(msg, j):
        return remote(
            pb.at[send_rows(msg, j), :], rb.at[send_rows(msg, j), :],
            push_send.at[msg, j], push_recv.at[msg, j], push_to[msg],
        )

    def weight_copy(msg):
        return remote(
            wsend.at[msg], wrecv.at[msg], wp_send.at[msg], wp_recv.at[msg], push_to[msg]
        )

    weight = jnp.full((8, 128), pw_ref[0], F32)
    share = weight * inv_den[:, :128]
    for msg in range(4):
        wsend[msg] = share * link[msg]
    for msg in range(3):
        weight_copy(msg).start()

    def push_first(j, carry):
        cols = rows(j * CH, CH)
        gradient = dot_nn(ot[...], cotb[:, cols])
        half_step = numb[:, cols].astype(F32) - STEP_SIZE * gradient
        acc[rows(j * 256, 256), :] = half_step * kept
        sending = half_step * inv_den
        for msg in range(4):
            pb[send_rows(msg, j), :] = (sending * link[msg]).astype(BF)
        for msg in range(3):
            push_copy(msg, j).start()
        return carry

    lax.fori_loop(0, NCH, push_first, 0)

    for msg in range(2):
        weight_copy(msg).wait_recv()
    wsend[3] = wsend[3] + wrecv[0] * carry_1 + wrecv[1] * carry_2
    weight_copy(3).start()

    def push_second(j, carry):
        for msg in range(2):
            push_copy(msg, j).wait_recv()
        one = rb[send_rows(0, j), :].astype(F32)
        two = rb[send_rows(1, j), :].astype(F32)
        four = pb[send_rows(3, j), :].astype(F32)
        pb[send_rows(3, j), :] = (four + one * carry_1 + two * carry_2).astype(BF)
        push_copy(3, j).start()
        part = rows(j * 256, 256)
        acc[part, :] = acc[part, :] + one * from_1 + two * from_2
        return carry

    lax.fori_loop(0, NCH, push_second, 0)

    for msg in range(2, 4):
        weight_copy(msg).wait_recv()
    w_out[...] = (
        weight * kept[:, :128] + wrecv[0] * from_1 + wrecv[1] * from_2 + wrecv[2] + wrecv[3]
    )

    def mix_copy(j):
        cols = rows(j * CH, CH)
        return pltpu.make_async_copy(mixb.at[:, cols], mix_out.at[:, cols], mix_sem.at[j])

    def push_third(j, carry):
        for msg in range(2, 4):
            push_copy(msg, j).wait_recv()
        eight = rb[send_rows(2, j), :].astype(F32)
        four = rb[send_rows(3, j), :].astype(F32)
        mixb[:, rows(j * CH, CH)] = (acc[rows(j * 256, 256), :] + eight + four).astype(BF)
        mix_copy(j).start()
        return carry

    lax.fori_loop(0, NCH, push_third, 0)

    def wait_mix(j, carry):
        mix_copy(j).wait()
        for msg in range(4):
            push_copy(msg, j).wait_send()
        return carry

    lax.fori_loop(0, NCH, wait_mix, 0)
    for msg in range(4):
        weight_copy(msg).wait_send()

    def wait_ring(s, carry):
        for sub in range(2):
            sib_copy(s, sub).wait_send()

            @pl.when(s < 7)
            def _():
                ring_copy(s, sub).wait_send()

        return carry

    lax.fori_loop(0, 8, wait_ring, 0)

    def wait_out(step, carry):
        dst = mod(me + step, 16)
        src = mod(me - step + 16, 16)
        for t in range(3):
            in_copy(t, dst, src).wait_send()
            out_copy(t, dst, src).wait_send()
            out_copy(t, dst, src).wait_recv()
        return carry

    lax.fori_loop(1, 16, wait_out, 0)
    for t in range(3):
        out_own(t).wait()


def body(
    queries, key_rows, value_rows, cotangent, numerators, push_weights, doc_ids, out_links,
    denominators,
):
    any_space = pl.BlockSpec(memory_space=pl.ANY)
    in_vmem = pl.BlockSpec(memory_space=pltpu.VMEM)
    in_smem = pl.BlockSpec(memory_space=pltpu.SMEM)
    dma = pltpu.SemaphoreType.DMA
    dq, dk, dv, mixed, weights = pl.pallas_call(
        kernel,
        out_shape=(
            jax.ShapeDtypeStruct((TOK, 16 * FW), BF),
            jax.ShapeDtypeStruct((TOK, 16 * FW), BF),
            jax.ShapeDtypeStruct((TOK, 16 * FW), BF),
            jax.ShapeDtypeStruct((FW, OUTW), BF),
            jax.ShapeDtypeStruct((8, 128), F32),
        ),
        in_specs=[any_space] * 5 + [in_vmem] + [in_smem] * 3,
        out_specs=(any_space,) * 4 + (in_vmem,),
        scratch_shapes=[
            pltpu.VMEM((SEQ, FW), BF),
            pltpu.VMEM((PAD + SEQ, FW), BF),
            pltpu.VMEM((PAD + SEQ, FW), BF),
            pltpu.VMEM((FW, PAD + SEQ), BF),
            pltpu.VMEM((FW, PAD + SEQ), BF),
            pltpu.VMEM((16 * WIN * 256, 256), BF),
            pltpu.VMEM((2, WIN * 256, 256), F32),
            pltpu.VMEM((FW, SEQ), BF),
            pltpu.VMEM((SEQ, OUTW), BF),
            pltpu.VMEM((FW, OUTW), BF),
            pltpu.VMEM((FW, OUTW), BF),
            pltpu.VMEM((2 * (PAD + SEQ), FW), F32),
            pltpu.VMEM((SEQ, FW), BF),
            pltpu.VMEM((SEQ, FW), BF),
            pltpu.VMEM((SEQ, FW), BF),
            pltpu.VMEM((PAD + SEQ, 128), F32),
            pltpu.VMEM((4 * NCH * 256, 256), BF),
            pltpu.VMEM((FW, OUTW), BF),
            pltpu.VMEM((4, 8, 128), F32),
            pltpu.VMEM((4, 8, 128), F32),
            dma((8,)),
            dma((3, 16)),
            dma((3, 16)),
            dma((8, 2)),
            dma((8, 2)),
            dma((8, 2)),
            dma((8, 2)),
            dma((3, 16)),
            dma((3, 16)),
            dma((4, NCH)),
            dma((4, NCH)),
            dma((4,)),
            dma((4,)),
            dma((NCH,)),
        ],
        compiler_params=pltpu.CompilerParams(
            collective_id=0, has_side_effects=True, vmem_limit_bytes=63 * 1024 * 1024
        ),
        name="push_step",
    )(
        queries[0], key_rows[0], value_rows[0], cotangent[0], numerators[0], doc_ids,
        push_weights, out_links, denominators,
    )
    return (dq[None], dk[None], dv[None], mixed[None], weights[0, :1])


def solution(mesh):
    tokens = P("rep", "seq", None)
    return jax.shard_map(
        body,
        mesh=mesh,
        in_specs=(tokens,) * 5 + (P("rep"), P("rep", None), P(), P()),
        out_specs=(tokens,) * 4 + (P("rep"),),
        check_vma=False,
    )
```

```python
import math

import jax
import jax.numpy as jnp
from jax import lax
from jax.experimental import pallas as pl
from jax.experimental.pallas import tpu as pltpu
from jax.sharding import PartitionSpec as P

HD = 128
SEQ = 2048
TOK = 128
OUTW = 3584
FW = 256
REACH = 4
WIN = REACH + 1
PAD = REACH * 256
CH = 256
NCH = OUTW // CH
HALF = OUTW // 2
STEP_SIZE = 3.0
SCALE = 1.0 / math.sqrt(HD)
EXP2_SCALE = SCALE * math.log2(math.e)
NEG = -1e30
MESH = pl.DeviceIdType.MESH
BF = jnp.bfloat16
F32 = jnp.float32


def mod(a, n):
    return lax.rem(a, n)


def dot_nn(a, b):
    return lax.dot_general(a, b, (((1,), (0,)), ((), ())), preferred_element_type=F32)


def dot_nt(a, b):
    return lax.dot_general(a, b, (((1,), (1,)), ((), ())), preferred_element_type=F32)


def rows(start, size):
    return pl.ds(pl.multiple_of(start, size), size)


def kernel(
    q_ref, k_ref, v_ref, cot_ref, num_ref, doc_ref, pw_ref, links_ref, den_ref,
    dq_out, dk_out, dv_out, mix_out, w_out,
    qh, kp, vp, kt, vt, pb, sbuf, ot, cotb, numb, debt, acc, base, dqb, dvb, dcol,
    outgo, rb, relay, wsend, wrecv,
    loc_sem, in_send, in_recv, ring_send, ring_recv, sib_send, sib_recv,
    out_send, out_recv, push_send, push_recv, relay_send, relay_recv, wp_send, wp_recv, mix_sem,
):
    rep = lax.axis_index("rep")
    me = lax.axis_index("seq")
    x, y = lax.div(rep, 4), mod(rep, 4)
    z, core = lax.div(me, 2), mod(me, 2)
    way = 1 - 2 * core
    sibling = (rep, z * 2 + 1 - core)
    ring_next = (rep, mod(z + way + 8, 8) * 2 + core)

    def at_xy(dx, dy):
        return (mod(x + dx + 4, 4) * 4 + mod(y + dy + 4, 4), me)

    push_to = (at_xy(0, 1), at_xy(0, 2), at_xy(2, 0), at_xy(1, 0))
    relay_to = (at_xy(0, -1), at_xy(-1, 0))

    barrier = pltpu.get_barrier_semaphore()
    for step in range(1, 16):
        pl.semaphore_signal(
            barrier, inc=1, device_id=(rep, mod(me + step, 16)), device_id_type=MESH
        )
    for dx, dy in ((0, 1), (0, 2), (0, 3), (1, 0), (2, 0), (3, 0)):
        pl.semaphore_signal(barrier, inc=1, device_id=at_xy(dx, dy), device_id_type=MESH)
    pl.semaphore_wait(barrier, 21)

    def remote(src, dst, send, recv, device):
        return pltpu.make_async_remote_copy(
            src_ref=src, dst_ref=dst, send_sem=send, recv_sem=recv, device_id=device,
            device_id_type=MESH,
        )

    heads_in = ((q_ref, qh, 0), (k_ref, kp, PAD), (v_ref, vp, PAD))

    def in_copy(t, dst, src):
        source, target, base = heads_in[t]
        return remote(
            source.at[:, rows(dst * FW, FW)],
            target.at[pl.ds(pl.multiple_of(base + src * TOK, TOK), TOK), :],
            in_send.at[t, dst], in_recv.at[t, src], (rep, dst),
        )

    def in_own(t):
        source, target, base = heads_in[t]
        return pltpu.make_async_copy(
            source.at[:, rows(me * FW, FW)],
            target.at[pl.ds(pl.multiple_of(base + me * TOK, TOK), TOK), :],
            loc_sem.at[t],
        )

    own_cot = pltpu.make_async_copy(cot_ref, cotb.at[rows(me * TOK, TOK), :], loc_sem.at[3])
    own_num = pltpu.make_async_copy(num_ref, numb, loc_sem.at[4])

    def send_in(step, carry):
        dst = mod(me + step, 16)
        for t in range(3):
            in_copy(t, dst, me).start()
        return carry

    own_num.start()
    own_cot.start()
    def ring_block(step):
        return mod(z - way * step + 8, 8) * 2 + core

    def sib_block(step):
        return mod(z + way * step + 8, 8) * 2 + 1 - core

    def piece(part, block, sub):
        return cotb.at[
            pl.ds(pl.multiple_of(block * TOK + sub * 64, 64), 64),
            part * HALF:(part + 1) * HALF,
        ]

    def ring_copy(part, step, sub):
        ref = piece(part, ring_block(step), sub)
        return remote(
            ref, ref, ring_send.at[part, step, sub], ring_recv.at[part, step + 1, sub], ring_next
        )

    def ring_arrival(part, step, sub):
        ref = piece(part, ring_block(step), sub)
        return remote(
            ref, ref, ring_send.at[part, step, sub], ring_recv.at[part, step, sub], ring_next
        )

    def sib_copy(part, step, sub):
        ref = piece(part, ring_block(step), sub)
        return remote(
            ref, ref, sib_send.at[part, step, sub], sib_recv.at[part, step, sub], sibling
        )

    def sib_arrival(part, step, sub):
        ref = piece(part, sib_block(step), sub)
        return remote(
            ref, ref, sib_send.at[part, step, sub], sib_recv.at[part, step, sub], sibling
        )

    def first_sends(part):
        for sub in range(2):
            ring_copy(part, 0, sub).start()
            sib_copy(part, 0, sub).start()

    def take(part, step):
        for sub in range(2):
            ring_arrival(part, step, sub).wait_recv()

            @pl.when(step < 7)
            def _():
                ring_copy(part, step, sub).start()

            sib_copy(part, step, sub).start()

    lax.fori_loop(1, 16, send_in, 0)
    for t in range(3):
        in_own(t).start()
    own_cot.wait()
    first_sends(0)

    kp[0:PAD, :] = jnp.zeros((PAD, FW), BF)
    vp[0:PAD, :] = jnp.zeros((PAD, FW), BF)
    dcol[0:PAD, :] = jnp.full((PAD, 128), -1.0, F32)

    def zero_acc(i, carry):
        acc[rows(i * 256, 256), :] = jnp.zeros((256, FW), F32)
        return carry

    lax.fori_loop(0, acc.shape[0] // 256, zero_acc, 0)

    def doc_columns(i, carry):
        part = doc_ref[:, rows(i * 128, 128)].astype(F32)
        dcol[pl.ds(pl.multiple_of(PAD + i * 128, 128), 128), :] = jnp.broadcast_to(
            part, (128, 128)
        ).T
        return carry

    lax.fori_loop(0, SEQ // 128, doc_columns, 0)
    own_num.wait()
    inv_weight = 1.0 / jnp.full((1, CH), pw_ref[0], F32)

    def debias(j, carry):
        cols = rows(j * CH, CH)
        debt[cols, :] = (numb[:, cols].astype(F32) * inv_weight).T.astype(BF)
        return carry

    lax.fori_loop(0, NCH, debias, 0)

    link = [links_ref[rep, mod(rep + off, 16)].astype(F32) for off in (1, 2, 8, 4)]
    inv_den = 1.0 / jnp.full((1, CH), den_ref[rep].astype(F32), F32)
    links_out = links_ref[rep, 0]
    for col in range(1, 16):
        links_out = links_out + links_ref[rep, col]
    kept = 1.0 - jnp.full((1, CH), links_out.astype(F32), F32) * inv_den
    def taken(dx, dy, off):
        source = at_xy(dx, dy)[0]
        return links_ref[source, mod(source + off, 16)].astype(F32)

    taken_1, taken_2, taken_8 = taken(0, -1, 1), taken(0, -2, 2), taken(-2, 0, 8)
    from_1 = jnp.where(y >= 1, 1.0, 0.0)
    from_2 = jnp.where(y >= 2, 1.0, 0.0)
    carry_1 = jnp.where(y == 0, 1.0, 0.0)
    carry_2 = jnp.where(y <= 1, 1.0, 0.0)

    def weight_copy(msg):
        return remote(
            wsend.at[msg], wrecv.at[msg], wp_send.at[msg], wp_recv.at[msg], push_to[msg]
        )

    weight = jnp.full((8, 128), pw_ref[0], F32)
    share = weight * inv_den[:, :128]
    for msg in range(4):
        wsend[msg] = share * link[msg]
    for msg in range(3):
        weight_copy(msg).start()

    for msg in range(2):
        weight_copy(msg).wait_recv()
    wsend[3] = wsend[3] + wrecv[0] * carry_1 + wrecv[1] * carry_2
    weight_copy(3).start()

    take(0, jnp.int32(1))

    def wait_in(step, carry):
        src = mod(me - step + 16, 16)
        for t in range(3):
            in_copy(t, mod(me + step, 16), src).wait_recv()
        return carry

    for t in range(3):
        in_own(t).wait()
    lax.fori_loop(1, 16, wait_in, 0)

    def flip(i, carry):
        cols = rows(i * 256, 256)
        kt[:, cols] = kp[cols, :].T
        vt[:, cols] = vp[cols, :].T
        return carry

    lax.fori_loop(0, (PAD + SEQ) // 256, flip, 0)

    later_key = lax.broadcasted_iota(jnp.int32, (256, 256), 0) <= lax.broadcasted_iota(
        jnp.int32, (256, 256), 1
    )

    def prob_rows(a, h, c):
        slot = mod(a - z + 14, 8)
        return rows(((slot * 2 + h) * WIN + c) * 256, 256)

    def forward(a):
        doc_q = doc_ref[:, rows(a * 256, 256)].astype(F32)
        for h in range(2):
            feats = slice(h * HD, (h + 1) * HD)
            qa = qh[rows(a * 256, 256), feats]
            peak = jnp.full((1, 256), NEG, F32)
            for c in range(WIN):
                keys = rows((a + c) * 256, 256)
                scores = dot_nt(kp[keys, feats], qa)
                dk_col = dcol[keys, :]
                allowed = jnp.concatenate([dk_col, dk_col], axis=1) == doc_q
                if c == REACH:
                    allowed = allowed & later_key
                scores = jnp.where(allowed, scores, NEG)
                sbuf[c * 256:(c + 1) * 256, :] = scores
                peak = jnp.maximum(peak, jnp.max(scores, axis=0, keepdims=True))
            total = jnp.zeros((1, 256), F32)
            for c in range(WIN):
                part = slice(c * 256, (c + 1) * 256)
                expo = jnp.exp2((sbuf[part, :] - peak) * EXP2_SCALE)
                sbuf[part, :] = expo
                total = total + jnp.sum(expo, axis=0, keepdims=True)
            inv_total = 1.0 / total
            out = jnp.zeros((HD, 256), F32)
            for c in range(WIN):
                probs = (sbuf[c * 256:(c + 1) * 256, :] * inv_total).astype(BF)
                pb[prob_rows(a, h, c), :] = probs
                out = out + dot_nn(vt[feats, rows((a + c) * 256, 256)], probs)
            ot[feats, rows(a * 256, 256)] = out.astype(BF)

    def out_copy(t, dst, src):
        source, target = ((dqb, dq_out), (qh, dk_out), (dvb, dv_out))[t]
        return remote(
            source.at[rows(dst * TOK, TOK), :], target.at[:, rows(src * FW, FW)],
            out_send.at[t, dst], out_recv.at[t, src], (rep, dst),
        )

    def out_own(t):
        source, target = ((dqb, dq_out), (qh, dk_out), (dvb, dv_out))[t]
        return pltpu.make_async_copy(
            source.at[rows(me * TOK, TOK), :], target.at[:, rows(me * FW, FW)], loc_sem.at[5 + t]
        )

    def backward(a, half, grad):
        tok = rows((a * 2 + half) * TOK, TOK)
        lanes = slice(half * TOK, (half + 1) * TOK)
        for h in range(2):
            feats = slice(h * HD, (h + 1) * HD)
            go = grad[lanes, feats]
            go_rows = go.T.astype(BF)
            go = go.astype(BF)
            centre = jnp.sum(
                go_rows.astype(F32) * ot[feats, tok].astype(F32), axis=0, keepdims=True
            )
            qa = qh[tok, feats]
            dq = jnp.zeros((HD, TOK), F32)
            for c in range(WIN):
                keys = rows((a + c) * 256, 256)
                probs = pb[prob_rows(a, h, c), lanes]
                grad_probs = dot_nn(vp[keys, feats], go_rows)
                grad_scores = (probs.astype(F32) * (grad_probs - centre)).astype(BF)
                v_rows = pl.ds(pl.multiple_of(PAD + SEQ + (a + c) * 256, 256), 256)
                acc[keys, feats] += dot_nn(grad_scores, qa)
                acc[v_rows, feats] += dot_nn(probs, go)
                dq = dq + dot_nn(kt[feats, keys], grad_scores)
            dqb[tok, feats] = (dq * SCALE).T.astype(BF)

    def block_of(step, half):
        return mod(z + (2 * half - 1) * step + 8, 8) * 2 + half

    def send_dq(step, half):
        device = block_of(step, half)

        @pl.when(device != me)
        def _():
            out_copy(0, device, me).start()

        @pl.when(device == me)
        def _():
            out_own(0).start()

    def compute(s):
        blocks = [block_of(s, half) for half in range(2)]
        both = jnp.concatenate([cotb[rows(b * TOK, TOK), :] for b in blocks], axis=0)
        grad = dot_nn(both, debt[...])
        for half in range(2):
            backward(lax.div(blocks[half], 2), half, grad)

    def forward_step(b, carry):
        forward(b)

        @pl.when(b <= 5)
        def _():
            take(0, b + 2)

        @pl.when(b == 4)
        def _():
            first_sends(1)

        return carry

    def wait_sib(part, step):
        for sub in range(2):
            sib_arrival(part, step, sub).wait_recv()

    def wait_sib_all(step, carry):
        wait_sib(0, step)
        return carry

    def ring_step(s, carry):
        @pl.when(s < 7)
        def _():
            take(1, s + 1)
            wait_sib(1, s)

        @pl.when(s == 3)
        def _():
            lax.fori_loop(0, NCH // 4, relay_step, 0)

        @pl.when(s == 6)
        def _():
            wait_sib(1, 7)
            lax.fori_loop(NCH // 2, NCH, push_first, 0)

        @pl.when(s == 7)
        def _():
            lax.fori_loop(0, NCH // 2, push_second, 0)

        compute(s)
        for half in range(2):
            send_dq(s, half)
        return carry

    def slot_rows(msg, j):
        return rows((msg * NCH + j) * 256, 256)

    def outgoing(msg, j):
        part = rows(j * 256, 256)
        return pb.at[part, :] if msg == 3 else outgo.at[part, :]

    def direct(msg, j):
        return remote(
            outgoing(msg, j), rb.at[slot_rows(msg, j), :],
            push_send.at[msg, j], push_recv.at[msg, j], push_to[msg],
        )

    def arrival(msg, j):
        return direct(msg, j)

    def relay_rows(way_round, i):
        return rows((way_round * (NCH // 2) + i) * 256, 256)

    def relay_in(way_round, i):
        return remote(
            outgoing(way_round + 1, 2 * i + 1), relay.at[relay_rows(way_round, i), :],
            push_send.at[way_round + 1, 2 * i + 1], relay_recv.at[way_round, i], relay_to[way_round],
        )

    def relay_on(way_round, i):
        return remote(
            relay.at[relay_rows(way_round, i), :], rb.at[slot_rows(way_round + 1, 2 * i + 1), :],
            relay_send.at[way_round, i], push_recv.at[way_round + 1, 2 * i + 1],
            relay_to[way_round],
        )

    def push_first(j, carry):
        cols = rows(j * CH, CH)
        gradient = dot_nn(ot[...], cotb[:, cols])
        half_step = numb[:, cols].astype(F32) - STEP_SIZE * gradient
        base[rows(j * 256, 256), :] = half_step * kept
        outgo[rows(j * 256, 256), :] = (half_step * inv_den).astype(BF)
        direct(0, j).start()

        @pl.when(mod(j, 2) == 0)
        def _():
            for way_round in range(2):
                direct(way_round + 1, j).start()

        @pl.when(mod(j, 2) == 1)
        def _():
            for way_round in range(2):
                relay_in(way_round, lax.div(j, 2)).start()

        return carry

    def relay_step(i, carry):
        for way_round in range(2):
            relay_in(way_round, i).wait_recv()
            relay_on(way_round, i).start()
        return carry

    def push_second(j, carry):
        for msg in range(2):
            arrival(msg, j).wait_recv()
        one = rb[slot_rows(0, j), :].astype(F32)
        two = rb[slot_rows(1, j), :].astype(F32)
        part = rows(j * 256, 256)
        four = outgo[part, :].astype(F32) * link[3]
        pb[part, :] = (four + one * (taken_1 * carry_1) + two * (taken_2 * carry_2)).astype(BF)
        direct(3, j).start()
        base[part, :] = base[part, :] + one * (taken_1 * from_1) + two * (taken_2 * from_2)
        return carry

    lax.fori_loop(0, 8, forward_step, 0)
    lax.fori_loop(0, 8, wait_sib_all, 0)
    lax.fori_loop(0, NCH // 2, push_first, 0)
    lax.fori_loop(0, 8, ring_step, 0)

    def finish(i, carry):
        dst = mod(me + i, 16)
        tok = rows(dst * TOK, TOK)
        qh[tok, :] = (
            acc[pl.ds(pl.multiple_of(PAD + dst * TOK, TOK), TOK), :] * SCALE
        ).astype(BF)
        dvb[tok, :] = acc[
            pl.ds(pl.multiple_of(2 * PAD + SEQ + dst * TOK, TOK), TOK), :
        ].astype(BF)

        @pl.when(i > 0)
        def _():
            out_copy(1, dst, me).start()
            out_copy(2, dst, me).start()

        @pl.when(i == 0)
        def _():
            out_own(1).start()
            out_own(2).start()

        return carry

    lax.fori_loop(0, 16, finish, 0)

    lax.fori_loop(NCH // 4, NCH // 2, relay_step, 0)
    lax.fori_loop(NCH // 2, NCH, push_second, 0)

    for msg in range(2, 4):
        weight_copy(msg).wait_recv()
    w_out[...] = (
        weight * kept[:, :128] + wrecv[0] * from_1 + wrecv[1] * from_2 + wrecv[2] + wrecv[3]
    )

    def mix_copy(j):
        cols = rows(j * CH, CH)
        return pltpu.make_async_copy(numb.at[:, cols], mix_out.at[:, cols], mix_sem.at[j])

    def push_third(j, carry):
        for msg in range(2, 4):
            arrival(msg, j).wait_recv()
        eight = rb[slot_rows(2, j), :].astype(F32)
        four = rb[slot_rows(3, j), :].astype(F32)
        numb[:, rows(j * CH, CH)] = (
            base[rows(j * 256, 256), :] + eight * taken_8 + four
        ).astype(BF)
        mix_copy(j).start()
        return carry

    lax.fori_loop(0, NCH, push_third, 0)

    def wait_mix(j, carry):
        mix_copy(j).wait()
        for msg in range(4):
            direct(msg, j).wait_send()
        return carry

    lax.fori_loop(0, NCH, wait_mix, 0)

    def wait_relay(i, carry):
        for way_round in range(2):
            relay_on(way_round, i).wait_send()
        return carry

    lax.fori_loop(0, NCH // 2, wait_relay, 0)
    for msg in range(4):
        weight_copy(msg).wait_send()

    def wait_ring(s, carry):
        for part in range(2):
            for sub in range(2):
                sib_copy(part, s, sub).wait_send()

                @pl.when(s < 7)
                def _():
                    ring_copy(part, s, sub).wait_send()

        return carry

    lax.fori_loop(0, 8, wait_ring, 0)

    def wait_out(step, carry):
        dst = mod(me + step, 16)
        src = mod(me - step + 16, 16)
        for t in range(3):
            in_copy(t, dst, src).wait_send()
            out_copy(t, dst, src).wait_send()
            out_copy(t, dst, src).wait_recv()
        return carry

    lax.fori_loop(1, 16, wait_out, 0)
    for t in range(3):
        out_own(t).wait()


def body(
    queries, key_rows, value_rows, cotangent, numerators, push_weights, doc_ids, out_links,
    denominators,
):
    any_space = pl.BlockSpec(memory_space=pl.ANY)
    in_vmem = pl.BlockSpec(memory_space=pltpu.VMEM)
    in_smem = pl.BlockSpec(memory_space=pltpu.SMEM)
    dma = pltpu.SemaphoreType.DMA
    dq, dk, dv, mixed, weights = pl.pallas_call(
        kernel,
        out_shape=(
            jax.ShapeDtypeStruct((TOK, 16 * FW), BF),
            jax.ShapeDtypeStruct((TOK, 16 * FW), BF),
            jax.ShapeDtypeStruct((TOK, 16 * FW), BF),
            jax.ShapeDtypeStruct((FW, OUTW), BF),
            jax.ShapeDtypeStruct((8, 128), F32),
        ),
        in_specs=[any_space] * 5 + [in_vmem] + [in_smem] * 3,
        out_specs=(any_space,) * 4 + (in_vmem,),
        scratch_shapes=[
            pltpu.VMEM((SEQ, FW), BF),
            pltpu.VMEM((PAD + SEQ, FW), BF),
            pltpu.VMEM((PAD + SEQ, FW), BF),
            pltpu.VMEM((FW, PAD + SEQ), BF),
            pltpu.VMEM((FW, PAD + SEQ), BF),
            pltpu.VMEM((16 * WIN * 256, 256), BF),
            pltpu.VMEM((WIN * 256, 256), F32),
            pltpu.VMEM((FW, SEQ), BF),
            pltpu.VMEM((SEQ, OUTW), BF),
            pltpu.VMEM((FW, OUTW), BF),
            pltpu.VMEM((OUTW, FW), BF),
            pltpu.VMEM((2 * (PAD + SEQ), FW), F32),
            pltpu.VMEM((NCH * 256, 256), F32),
            pltpu.VMEM((SEQ, FW), BF),
            pltpu.VMEM((SEQ, FW), BF),
            pltpu.VMEM((PAD + SEQ, 128), F32),
            pltpu.VMEM((NCH * 256, 256), BF),
            pltpu.VMEM((4 * NCH * 256, 256), BF),
            pltpu.VMEM((NCH * 256, 256), BF),
            pltpu.VMEM((4, 8, 128), F32),
            pltpu.VMEM((4, 8, 128), F32),
            dma((8,)),
            dma((3, 16)),
            dma((3, 16)),
            dma((2, 8, 2)),
            dma((2, 8, 2)),
            dma((2, 8, 2)),
            dma((2, 8, 2)),
            dma((3, 16)),
            dma((3, 16)),
            dma((4, NCH)),
            dma((4, NCH)),
            dma((2, NCH // 2)),
            dma((2, NCH // 2)),
            dma((4,)),
            dma((4,)),
            dma((NCH,)),
        ],
        compiler_params=pltpu.CompilerParams(
            collective_id=0, has_side_effects=True, vmem_limit_bytes=63 * 1024 * 1024
        ),
        name="push_step",
    )(
        queries[0], key_rows[0], value_rows[0], cotangent[0], numerators[0], doc_ids,
        push_weights, out_links, denominators,
    )
    return (dq[None], dk[None], dv[None], mixed[None], weights[0, :1])


def solution(mesh):
    tokens = P("rep", "seq", None)
    return jax.shard_map(
        body,
        mesh=mesh,
        in_specs=(tokens,) * 5 + (P("rep"), P("rep", None), P(), P()),
        out_specs=(tokens,) * 4 + (P("rep"),),
        check_vma=False,
    )
```

```python
import math

import jax
import jax.numpy as jnp
from jax import lax
from jax.experimental import pallas as pl
from jax.experimental.pallas import tpu as pltpu
from jax.sharding import PartitionSpec as P

HD = 128
SEQ = 2048
TOK = 128
OUTW = 3584
FW = 256
REACH = 4
WIN = REACH + 1
PAD = REACH * 256
CH = 256
NCH = OUTW // CH
FIRST = 5
HALF = FIRST * CH
COLS = (slice(0, HALF), slice(HALF, OUTW))
STEP_SIZE = 3.0
SCALE = 1.0 / math.sqrt(HD)
EXP2_SCALE = SCALE * math.log2(math.e)
NEG = -1e30
MESH = pl.DeviceIdType.MESH
BF = jnp.bfloat16
F32 = jnp.float32


def mod(a, n):
    return lax.rem(a, n)


def dot_nn(a, b):
    return lax.dot_general(a, b, (((1,), (0,)), ((), ())), preferred_element_type=F32)


def dot_nt(a, b):
    return lax.dot_general(a, b, (((1,), (1,)), ((), ())), preferred_element_type=F32)


def rows(start, size):
    return pl.ds(pl.multiple_of(start, size), size)


def kernel(
    q_ref, k_ref, v_ref, cot_ref, num_ref, doc_ref, pw_ref, links_ref, den_ref,
    dq_out, dk_out, dv_out, mix_out, w_out,
    qh, kp, vp, kt, vt, pb, sbuf, ot, cotb, numb, debt, acc, base, dqb, part_grad, dcol,
    outgo, rb, relay, wsend, wrecv,
    loc_sem, in_send, in_recv, ring_send, ring_recv, sib_send, sib_recv,
    out_send, out_recv, push_send, push_recv, relay_send, relay_recv, wp_send, wp_recv, mix_sem,
):
    rep = lax.axis_index("rep")
    me = lax.axis_index("seq")
    x, y = lax.div(rep, 4), mod(rep, 4)
    z, core = lax.div(me, 2), mod(me, 2)
    way = 1 - 2 * core
    sibling = (rep, z * 2 + 1 - core)
    ring_next = (rep, mod(z + way + 8, 8) * 2 + core)

    def at_xy(dx, dy):
        return (mod(x + dx + 4, 4) * 4 + mod(y + dy + 4, 4), me)

    push_to = (at_xy(0, 1), at_xy(0, 2), at_xy(2, 0), at_xy(1, 0))
    relay_to = (at_xy(0, -1), at_xy(-1, 0))

    barrier = pltpu.get_barrier_semaphore()
    for step in range(1, 16):
        pl.semaphore_signal(
            barrier, inc=1, device_id=(rep, mod(me + step, 16)), device_id_type=MESH
        )
    for dx, dy in ((0, 1), (0, 2), (0, 3), (1, 0), (2, 0), (3, 0)):
        pl.semaphore_signal(barrier, inc=1, device_id=at_xy(dx, dy), device_id_type=MESH)
    pl.semaphore_wait(barrier, 21)

    def remote(src, dst, send, recv, device):
        return pltpu.make_async_remote_copy(
            src_ref=src, dst_ref=dst, send_sem=send, recv_sem=recv, device_id=device,
            device_id_type=MESH,
        )

    heads_in = ((q_ref, qh, 0), (k_ref, kp, PAD), (v_ref, vp, PAD))

    def in_copy(t, dst, src):
        source, target, base = heads_in[t]
        return remote(
            source.at[:, rows(dst * FW, FW)],
            target.at[pl.ds(pl.multiple_of(base + src * TOK, TOK), TOK), :],
            in_send.at[t, dst], in_recv.at[t, src], (rep, dst),
        )

    def in_own(t):
        source, target, base = heads_in[t]
        return pltpu.make_async_copy(
            source.at[:, rows(me * FW, FW)],
            target.at[pl.ds(pl.multiple_of(base + me * TOK, TOK), TOK), :],
            loc_sem.at[t],
        )

    own_cot = pltpu.make_async_copy(cot_ref, cotb.at[rows(me * TOK, TOK), :], loc_sem.at[3])
    own_num = pltpu.make_async_copy(num_ref, numb, loc_sem.at[4])

    def send_in(step, carry):
        dst = mod(me + step, 16)
        for t in range(3):
            in_copy(t, dst, me).start()
        return carry

    own_num.start()
    own_cot.start()
    def ring_block(step):
        return mod(z - way * step + 8, 8) * 2 + core

    def sib_block(step):
        return mod(z + way * step + 8, 8) * 2 + 1 - core

    def piece(part, block, sub):
        return cotb.at[
            pl.ds(pl.multiple_of(block * TOK + sub * 64, 64), 64),
            COLS[part],
        ]

    def ring_copy(part, step, sub):
        ref = piece(part, ring_block(step), sub)
        return remote(
            ref, ref, ring_send.at[part, step, sub], ring_recv.at[part, step + 1, sub], ring_next
        )

    def ring_arrival(part, step, sub):
        ref = piece(part, ring_block(step), sub)
        return remote(
            ref, ref, ring_send.at[part, step, sub], ring_recv.at[part, step, sub], ring_next
        )

    def sib_copy(part, step, sub):
        ref = piece(part, ring_block(step), sub)
        return remote(
            ref, ref, sib_send.at[part, step, sub], sib_recv.at[part, step, sub], sibling
        )

    def sib_arrival(part, step, sub):
        ref = piece(part, sib_block(step), sub)
        return remote(
            ref, ref, sib_send.at[part, step, sub], sib_recv.at[part, step, sub], sibling
        )

    def first_sends(part):
        for sub in range(2):
            ring_copy(part, 0, sub).start()
            sib_copy(part, 0, sub).start()

    def take(part, step):
        for sub in range(2):
            ring_arrival(part, step, sub).wait_recv()

            @pl.when(step < 7)
            def _():
                ring_copy(part, step, sub).start()

            sib_copy(part, step, sub).start()

    lax.fori_loop(1, 16, send_in, 0)
    for t in range(3):
        in_own(t).start()
    own_cot.wait()
    first_sends(0)

    kp[0:PAD, :] = jnp.zeros((PAD, FW), BF)
    vp[0:PAD, :] = jnp.zeros((PAD, FW), BF)
    dcol[0:PAD, :] = jnp.full((PAD, 128), -1.0, F32)

    def zero_acc(i, carry):
        acc[rows(i * 256, 256), :] = jnp.zeros((256, FW), F32)
        return carry

    lax.fori_loop(0, acc.shape[0] // 256, zero_acc, 0)

    def doc_columns(i, carry):
        part = doc_ref[:, rows(i * 128, 128)].astype(F32)
        dcol[pl.ds(pl.multiple_of(PAD + i * 128, 128), 128), :] = jnp.broadcast_to(
            part, (128, 128)
        ).T
        return carry

    lax.fori_loop(0, SEQ // 128, doc_columns, 0)
    own_num.wait()
    inv_weight = 1.0 / jnp.full((1, CH), pw_ref[0], F32)

    def debias(j, carry):
        cols = rows(j * CH, CH)
        debt[cols, :] = (numb[:, cols].astype(F32) * inv_weight).T.astype(BF)
        return carry

    lax.fori_loop(0, NCH, debias, 0)

    link = [links_ref[rep, mod(rep + off, 16)].astype(F32) for off in (1, 2, 8, 4)]
    inv_den = 1.0 / jnp.full((1, CH), den_ref[rep].astype(F32), F32)
    links_out = links_ref[rep, 0]
    for col in range(1, 16):
        links_out = links_out + links_ref[rep, col]
    kept = 1.0 - jnp.full((1, CH), links_out.astype(F32), F32) * inv_den
    def taken(dx, dy, off):
        source = at_xy(dx, dy)[0]
        return links_ref[source, mod(source + off, 16)].astype(F32)

    taken_1, taken_2, taken_8 = taken(0, -1, 1), taken(0, -2, 2), taken(-2, 0, 8)
    from_1 = jnp.where(y >= 1, 1.0, 0.0)
    from_2 = jnp.where(y >= 2, 1.0, 0.0)
    carry_1 = jnp.where(y == 0, 1.0, 0.0)
    carry_2 = jnp.where(y <= 1, 1.0, 0.0)

    def weight_copy(msg):
        return remote(
            wsend.at[msg], wrecv.at[msg], wp_send.at[msg], wp_recv.at[msg], push_to[msg]
        )

    weight = jnp.full((8, 128), pw_ref[0], F32)
    share = weight * inv_den[:, :128]
    for msg in range(4):
        wsend[msg] = share * link[msg]
    for msg in range(3):
        weight_copy(msg).start()

    for msg in range(2):
        weight_copy(msg).wait_recv()
    wsend[3] = wsend[3] + wrecv[0] * carry_1 + wrecv[1] * carry_2
    weight_copy(3).start()

    take(0, jnp.int32(1))

    def wait_in(step, carry):
        src = mod(me - step + 16, 16)
        for t in range(3):
            in_copy(t, mod(me + step, 16), src).wait_recv()
        return carry

    for t in range(3):
        in_own(t).wait()
    lax.fori_loop(1, 16, wait_in, 0)

    def flip(i, carry):
        cols = rows(i * 256, 256)
        kt[:, cols] = kp[cols, :].T
        vt[:, cols] = vp[cols, :].T
        return carry

    lax.fori_loop(0, (PAD + SEQ) // 256, flip, 0)

    later_key = lax.broadcasted_iota(jnp.int32, (256, 256), 0) <= lax.broadcasted_iota(
        jnp.int32, (256, 256), 1
    )

    def prob_rows(a, h, c):
        slot = mod(a - z + 14, 8)
        return rows(((slot * 2 + h) * WIN + c) * 256, 256)

    def forward(a):
        doc_q = doc_ref[:, rows(a * 256, 256)].astype(F32)
        for h in range(2):
            feats = slice(h * HD, (h + 1) * HD)
            qa = qh[rows(a * 256, 256), feats]
            peak = jnp.full((1, 256), NEG, F32)
            for c in range(WIN):
                keys = rows((a + c) * 256, 256)
                scores = dot_nt(kp[keys, feats], qa)
                dk_col = dcol[keys, :]
                allowed = jnp.concatenate([dk_col, dk_col], axis=1) == doc_q
                if c == REACH:
                    allowed = allowed & later_key
                scores = jnp.where(allowed, scores, NEG)
                sbuf[c * 256:(c + 1) * 256, :] = scores
                peak = jnp.maximum(peak, jnp.max(scores, axis=0, keepdims=True))
            total = jnp.zeros((1, 256), F32)
            for c in range(WIN):
                part = slice(c * 256, (c + 1) * 256)
                expo = jnp.exp2((sbuf[part, :] - peak) * EXP2_SCALE)
                sbuf[part, :] = expo
                total = total + jnp.sum(expo, axis=0, keepdims=True)
            inv_total = 1.0 / total
            out = jnp.zeros((HD, 256), F32)
            for c in range(WIN):
                probs = (sbuf[c * 256:(c + 1) * 256, :] * inv_total).astype(BF)
                pb[prob_rows(a, h, c), :] = probs
                out = out + dot_nn(vt[feats, rows((a + c) * 256, 256)], probs)
            ot[feats, rows(a * 256, 256)] = out.astype(BF)

    def out_copy(t, dst, src):
        source, target = ((dqb, dq_out), (qh, dk_out), (kp, dv_out))[t]
        return remote(
            source.at[rows(dst * TOK, TOK), :], target.at[:, rows(src * FW, FW)],
            out_send.at[t, dst], out_recv.at[t, src], (rep, dst),
        )

    def out_own(t):
        source, target = ((dqb, dq_out), (qh, dk_out), (kp, dv_out))[t]
        return pltpu.make_async_copy(
            source.at[rows(me * TOK, TOK), :], target.at[:, rows(me * FW, FW)], loc_sem.at[5 + t]
        )

    def backward(a, half, grad):
        tok = rows((a * 2 + half) * TOK, TOK)
        lanes = slice(half * TOK, (half + 1) * TOK)
        for h in range(2):
            feats = slice(h * HD, (h + 1) * HD)
            go = grad[lanes, feats]
            go_rows = go.T.astype(BF)
            go = go.astype(BF)
            centre = jnp.sum(
                go_rows.astype(F32) * ot[feats, tok].astype(F32), axis=0, keepdims=True
            )
            qa = qh[tok, feats]
            dq = jnp.zeros((HD, TOK), F32)
            for c in range(WIN):
                keys = rows((a + c) * 256, 256)
                probs = pb[prob_rows(a, h, c), lanes]
                grad_probs = dot_nn(vp[keys, feats], go_rows)
                grad_scores = (probs.astype(F32) * (grad_probs - centre)).astype(BF)
                v_rows = pl.ds(pl.multiple_of(PAD + SEQ + (a + c) * 256, 256), 256)
                acc[keys, feats] += dot_nn(grad_scores, qa)
                acc[v_rows, feats] += dot_nn(probs, go)
                dq = dq + dot_nn(kt[feats, keys], grad_scores)
            dqb[tok, feats] = (dq * SCALE).T.astype(BF)

    def block_of(step, half):
        return mod(z + (2 * half - 1) * step + 8, 8) * 2 + half

    def send_dq(step, half):
        device = block_of(step, half)

        @pl.when(device != me)
        def _():
            out_copy(0, device, me).start()

        @pl.when(device == me)
        def _():
            out_own(0).start()

    def both_blocks(step, part):
        return jnp.concatenate(
            [
                cotb[rows(block_of(step, half) * TOK, TOK), COLS[part]]
                for half in range(2)
            ],
            axis=0,
        )

    def compute(s):
        grad = part_grad[rows(s * 256, 256), :] + dot_nn(both_blocks(s, 1), debt[HALF:OUTW, :])
        for half in range(2):
            backward(lax.div(block_of(s, half), 2), half, grad)

    def forward_step(b, carry):
        forward(b)

        @pl.when(b <= 5)
        def _():
            take(0, b + 2)

        @pl.when(b == 4)
        def _():
            first_sends(1)

        wait_sib(0, b)
        part_grad[rows(b * 256, 256), :] = dot_nn(both_blocks(b, 0), debt[0:HALF, :])
        return carry

    def wait_sib(part, step):
        for sub in range(2):
            sib_arrival(part, step, sub).wait_recv()

    def ring_step(s, carry):
        @pl.when(s < 7)
        def _():
            take(1, s + 1)
            wait_sib(1, s)

        @pl.when(s == 2)
        def _():
            lax.fori_loop(0, FIRST // 2, relay_step, 0)

        @pl.when(s == 5)
        def _():
            lax.fori_loop(0, FIRST, push_second, 0)

        @pl.when(s == 6)
        def _():
            wait_sib(1, 7)
            lax.fori_loop(FIRST, NCH, push_first, 0)

        compute(s)
        for half in range(2):
            send_dq(s, half)
        return carry

    def slot_rows(msg, j):
        return rows((msg * NCH + j) * 256, 256)

    def joined_rows(j):
        return rows((j + jnp.where(j < FIRST, 2 * 2 * WIN, -FIRST)) * 256, 256)

    def outgoing(msg, j):
        if msg == 3:
            return pb.at[joined_rows(j), :]
        return outgo.at[rows(j * 256, 256), :]

    def direct(msg, j):
        return remote(
            outgoing(msg, j), rb.at[slot_rows(msg, j), :],
            push_send.at[msg, j], push_recv.at[msg, j], push_to[msg],
        )

    def arrival(msg, j):
        return direct(msg, j)

    def relay_rows(way_round, i):
        return rows((way_round * (NCH // 2) + i) * 256, 256)

    def relay_in(way_round, i):
        return remote(
            outgoing(way_round + 1, 2 * i + 1), relay.at[relay_rows(way_round, i), :],
            push_send.at[way_round + 1, 2 * i + 1], relay_recv.at[way_round, i], relay_to[way_round],
        )

    def relay_on(way_round, i):
        return remote(
            relay.at[relay_rows(way_round, i), :], rb.at[slot_rows(way_round + 1, 2 * i + 1), :],
            relay_send.at[way_round, i], push_recv.at[way_round + 1, 2 * i + 1],
            relay_to[way_round],
        )

    def push_first(j, carry):
        cols = rows(j * CH, CH)
        gradient = dot_nn(ot[...], cotb[:, cols])
        half_step = numb[:, cols].astype(F32) - STEP_SIZE * gradient
        base[rows(j * 256, 256), :] = half_step * kept
        outgo[rows(j * 256, 256), :] = (half_step * inv_den).astype(BF)
        direct(0, j).start()

        @pl.when(mod(j, 2) == 0)
        def _():
            for way_round in range(2):
                direct(way_round + 1, j).start()

        @pl.when(mod(j, 2) == 1)
        def _():
            for way_round in range(2):
                relay_in(way_round, lax.div(j, 2)).start()

        return carry

    def relay_step(i, carry):
        for way_round in range(2):
            relay_in(way_round, i).wait_recv()
            relay_on(way_round, i).start()
        return carry

    def push_second(j, carry):
        for msg in range(2):
            arrival(msg, j).wait_recv()
        one = rb[slot_rows(0, j), :].astype(F32)
        two = rb[slot_rows(1, j), :].astype(F32)
        part = rows(j * 256, 256)
        four = outgo[part, :].astype(F32) * link[3]
        pb[joined_rows(j), :] = (four + one * (taken_1 * carry_1) + two * (taken_2 * carry_2)).astype(BF)
        direct(3, j).start()
        base[part, :] = base[part, :] + one * (taken_1 * from_1) + two * (taken_2 * from_2)
        return carry

    lax.fori_loop(0, 8, forward_step, 0)
    lax.fori_loop(0, FIRST, push_first, 0)
    lax.fori_loop(0, 8, ring_step, 0)

    def finish(i, carry):
        dst = mod(me + i, 16)
        tok = rows(dst * TOK, TOK)
        qh[tok, :] = (
            acc[pl.ds(pl.multiple_of(PAD + dst * TOK, TOK), TOK), :] * SCALE
        ).astype(BF)
        kp[tok, :] = acc[
            pl.ds(pl.multiple_of(2 * PAD + SEQ + dst * TOK, TOK), TOK), :
        ].astype(BF)

        @pl.when(i > 0)
        def _():
            out_copy(1, dst, me).start()
            out_copy(2, dst, me).start()

        @pl.when(i == 0)
        def _():
            out_own(1).start()
            out_own(2).start()

        return carry

    lax.fori_loop(0, 16, finish, 0)

    lax.fori_loop(FIRST // 2, NCH // 2, relay_step, 0)
    lax.fori_loop(FIRST, NCH, push_second, 0)

    for msg in range(2, 4):
        weight_copy(msg).wait_recv()
    w_out[...] = (
        weight * kept[:, :128] + wrecv[0] * from_1 + wrecv[1] * from_2 + wrecv[2] + wrecv[3]
    )

    def mix_copy(j):
        cols = rows(j * CH, CH)
        return pltpu.make_async_copy(numb.at[:, cols], mix_out.at[:, cols], mix_sem.at[j])

    def push_third(j, carry):
        for msg in range(2, 4):
            arrival(msg, j).wait_recv()
        eight = rb[slot_rows(2, j), :].astype(F32)
        four = rb[slot_rows(3, j), :].astype(F32)
        numb[:, rows(j * CH, CH)] = (
            base[rows(j * 256, 256), :] + eight * taken_8 + four
        ).astype(BF)
        mix_copy(j).start()
        return carry

    lax.fori_loop(0, NCH, push_third, 0)

    def wait_mix(j, carry):
        mix_copy(j).wait()
        for msg in range(4):
            direct(msg, j).wait_send()
        return carry

    lax.fori_loop(0, NCH, wait_mix, 0)

    def wait_relay(i, carry):
        for way_round in range(2):
            relay_on(way_round, i).wait_send()
        return carry

    lax.fori_loop(0, NCH // 2, wait_relay, 0)
    for msg in range(4):
        weight_copy(msg).wait_send()

    def wait_ring(s, carry):
        for part in range(2):
            for sub in range(2):
                sib_copy(part, s, sub).wait_send()

                @pl.when(s < 7)
                def _():
                    ring_copy(part, s, sub).wait_send()

        return carry

    lax.fori_loop(0, 8, wait_ring, 0)

    def wait_out(step, carry):
        dst = mod(me + step, 16)
        src = mod(me - step + 16, 16)
        for t in range(3):
            in_copy(t, dst, src).wait_send()
            out_copy(t, dst, src).wait_send()
            out_copy(t, dst, src).wait_recv()
        return carry

    lax.fori_loop(1, 16, wait_out, 0)
    for t in range(3):
        out_own(t).wait()


def body(
    queries, key_rows, value_rows, cotangent, numerators, push_weights, doc_ids, out_links,
    denominators,
):
    any_space = pl.BlockSpec(memory_space=pl.ANY)
    in_vmem = pl.BlockSpec(memory_space=pltpu.VMEM)
    in_smem = pl.BlockSpec(memory_space=pltpu.SMEM)
    dma = pltpu.SemaphoreType.DMA
    dq, dk, dv, mixed, weights = pl.pallas_call(
        kernel,
        out_shape=(
            jax.ShapeDtypeStruct((TOK, 16 * FW), BF),
            jax.ShapeDtypeStruct((TOK, 16 * FW), BF),
            jax.ShapeDtypeStruct((TOK, 16 * FW), BF),
            jax.ShapeDtypeStruct((FW, OUTW), BF),
            jax.ShapeDtypeStruct((8, 128), F32),
        ),
        in_specs=[any_space] * 5 + [in_vmem] + [in_smem] * 3,
        out_specs=(any_space,) * 4 + (in_vmem,),
        scratch_shapes=[
            pltpu.VMEM((SEQ, FW), BF),
            pltpu.VMEM((PAD + SEQ, FW), BF),
            pltpu.VMEM((PAD + SEQ, FW), BF),
            pltpu.VMEM((FW, PAD + SEQ), BF),
            pltpu.VMEM((FW, PAD + SEQ), BF),
            pltpu.VMEM((16 * WIN * 256, 256), BF),
            pltpu.VMEM((WIN * 256, 256), F32),
            pltpu.VMEM((FW, SEQ), BF),
            pltpu.VMEM((SEQ, OUTW), BF),
            pltpu.VMEM((FW, OUTW), BF),
            pltpu.VMEM((OUTW, FW), BF),
            pltpu.VMEM((2 * (PAD + SEQ), FW), F32),
            pltpu.VMEM((NCH * 256, 256), F32),
            pltpu.VMEM((SEQ, FW), BF),
            pltpu.VMEM((SEQ, FW), F32),
            pltpu.VMEM((PAD + SEQ, 128), F32),
            pltpu.VMEM((NCH * 256, 256), BF),
            pltpu.VMEM((4 * NCH * 256, 256), BF),
            pltpu.VMEM((NCH * 256, 256), BF),
            pltpu.VMEM((4, 8, 128), F32),
            pltpu.VMEM((4, 8, 128), F32),
            dma((8,)),
            dma((3, 16)),
            dma((3, 16)),
            dma((2, 8, 2)),
            dma((2, 8, 2)),
            dma((2, 8, 2)),
            dma((2, 8, 2)),
            dma((3, 16)),
            dma((3, 16)),
            dma((4, NCH)),
            dma((4, NCH)),
            dma((2, NCH // 2)),
            dma((2, NCH // 2)),
            dma((4,)),
            dma((4,)),
            dma((NCH,)),
        ],
        compiler_params=pltpu.CompilerParams(
            collective_id=0, has_side_effects=True, vmem_limit_bytes=63 * 1024 * 1024
        ),
        name="push_step",
    )(
        queries[0], key_rows[0], value_rows[0], cotangent[0], numerators[0], doc_ids,
        push_weights, out_links, denominators,
    )
    return (dq[None], dk[None], dv[None], mixed[None], weights[0, :1])


def solution(mesh):
    tokens = P("rep", "seq", None)
    return jax.shard_map(
        body,
        mesh=mesh,
        in_specs=(tokens,) * 5 + (P("rep"), P("rep", None), P(), P()),
        out_specs=(tokens,) * 4 + (P("rep"),),
        check_vma=False,
    )
```
